32 devices in a mesh: member: 2 (over x), sub: 8 (over z, y), var: 2 (over core).
Axes of the slice: x: 2, y: 2, z: 4, core: 2. Of those that a mesh axis runs over, the one named last changes fastest.
Arguments:
- innovations: float32 [8, 65536], P('var', ('member', 'sub')), parts along dimension 1, may hold values from -6 to 6
- obs_owner: int32 [65536, 1], P(('member', 'sub')), parts along dimension 0, may hold values from 0 to 7; in each aligned block of 4096 rows (0 to 4095, 4096 to 8191, ...) at most 1024 rows name the same one
- obs_local: int32 [65536], P(('member', 'sub')), parts along dimension 0, may hold values from 0 to 2047
- obs_level: int32 [65536, 1], P(('member', 'sub')), parts along dimension 0, may hold values from 0 to 63; in each aligned block of 4096 rows (0 to 4095, 4096 to 8191, ...) at most 128 rows name the same one
- band_width: int32 [64], replicated, may hold values from 2 to 16
- vert_scale: float32 [8, 64], P('var'), may hold values from 1 to 4
- sigma: float32 [8, 64], P('var'), may hold values from 0.5 to 2
- balance: float32 [8, 8], P('var')
Outputs:
- increment: float32 [8, 64, 64, 512], P('var', None, ('member', 'sub')), parts along dimension 2
The draws below stay inside these ranges and needn't reach their ends.
There are 2 independent parts, one for each index of `member`. The reference program is written for one: setup_inputs(seed, part) draws one part's arguments, and reference() takes and returns one part's arrays. A program takes and returns all parts, laid end to end along the dimension named above; an argument that names none is the same for every part. Nothing has to cross between parts.
Inputs may be any that keep to these rules, and one draw needn't show every extreme that they name: `obs_owner`: in the rows of one device no subdomain is named more than 1024 times, a bound that some block reaches. `obs_level`: in the rows of one device no level is named more than 128 times, a bound that some block reaches.
All inputs are finite; a program needn't handle non-finite values.
Results may differ from the reference program's by a relative error of at most 0.00008.
Values sent between devices are 32-bit elements; how exact they have to be, the bound alone decides.
A program may use at most 192 MiB of HBM per device.

```python
import math
import jax
import jax.numpy as jnp
import numpy as np
from jax import lax

V = 8
LEV = 64
VB = 6
NX_DEV = 4
NY = 512
OBS_DEV = 4096
NX = 32
OBS = 32768
CAP = 1024
LCAP = 128
N_SUB = 8


def draw_balance(key, part):
    noise = jax.random.normal(key, (V, V), jnp.float32)
    index = jnp.arange(V)
    eye = (index[:, None] == index[None, :]).astype(jnp.float32)
    return eye + 0.3 * noise


def with_ends(drawn, stream_key, smallest, top_value):
    longest = drawn.shape.index(max(drawn.shape))
    spots = []
    for shift in (0, 1):
        where = [jax.random.randint(jax.random.fold_in(stream_key, axis), (), 0, length) for axis, length in enumerate(drawn.shape)]
        where[longest] = (where[longest] + shift) % drawn.shape[longest]
        spots.append(tuple(where))
    return drawn.at[spots[0]].set(smallest).at[spots[1]].set(top_value)


def block_levels(rng, dims, shards, low, largest):
    level, own = 1.0, jax.random.fold_in(rng, 6)
    for dim, shards_of in shards:
        heights = jnp.exp(jax.random.uniform(jax.random.fold_in(own, dim), (shards_of,), jnp.float32, low / len(shards), largest / len(shards)))
        level = level * jnp.repeat(heights, dims[dim] // shards_of).reshape([-1 if axis == dim else 1 for axis in range(len(dims))])
    return level


def deal_out(stream_key, own, number, rows, number_of, top, reach, skew):
    ranking = jax.random.permutation(stream_key, number_of)
    heavy_load, common = shares(number_of, rows * top, reach, skew, True), shares(number_of, rows * top, reach, skew, False)
    places = jnp.arange(number_of)

    def named(lengths, offset_by):
        used = int((lengths > 0).sum())
        fixed = max(1, used // 4)
        moved = fixed + (places - fixed + offset_by * (used - fixed)) % max(1, number_of - fixed)
        return jnp.zeros((number_of,), jnp.int32).at[ranking[jnp.where(places < fixed, places, moved)]].set(jnp.asarray(lengths, jnp.int32))

    lengths = jnp.where(number % 4 == 0, named(heavy_load, number // 4), named(common, number - number // 4 - 1))
    mixed = jax.random.permutation(jax.random.fold_in(own, 3), number_of)
    giver, receiver = mixed[0:number_of // 2 * 2:2], mixed[1:number_of // 2 * 2:2]
    room = jnp.minimum(lengths[giver] - 1, reach - lengths[receiver]) // 2
    room = jnp.where((giver == ranking[0]) | (receiver == ranking[0]) | (lengths[receiver] == 0), 0, jnp.maximum(room, 0))
    moved = jax.random.randint(jax.random.fold_in(own, 4), (number_of // 2,), 0, 1 << 20) % (room + 1)
    lengths = lengths.at[giver].add(-moved).at[receiver].add(moved)
    items = jnp.searchsorted(jnp.cumsum(lengths), jnp.arange(rows * top), side="right").astype(jnp.int32)
    grid = items.reshape(top, rows).T
    grid = grid[jax.random.permutation(jax.random.fold_in(own, 1), rows)]
    offset_by = jax.random.randint(jax.random.fold_in(own, 2), (rows, 1), 0, top)
    return jnp.take_along_axis(grid, (jnp.arange(top)[None, :] + offset_by) % top, axis=1)


def shares(amount, total, most, slope, full):
    loads = [(1 << 20) // math.isqrt(standing ** slope) + 1 for standing in range(1, amount + 1)]
    largest = most if full else min(most, max(-(-total // amount), total * loads[0] // sum(loads)))
    least = 1 if total - largest >= amount - 1 else 0
    holding, spare = [largest] + [least] * (amount - 1), total - largest - least * (amount - 1)
    while spare > 0:
        free = [i for i in range(1, amount) if holding[i] < largest] or [i for i in range(1, amount) if holding[i] < most]
        pool, remaining = sum([loads[i] for i in free]), spare
        for i in free:
            addition = min(most - holding[i], max(1, remaining * loads[i] // pool), spare)
            holding[i] = holding[i] + addition
            spare = spare - addition
    return np.array(holding)


def gaussian(stream_key, extent, scale, reach, split=(), held_as=jnp.bfloat16):
    factor_of = block_levels(stream_key, extent, split, -0.22, 0.18) if split else 1.0
    drawn = jax.random.normal(stream_key, extent, jnp.float32) * scale * factor_of
    return jnp.minimum(jnp.maximum(drawn, -reach), reach).astype(held_as)


def setup_inputs(seed: int = 0, part: int = 0) -> dict:
    streams_of = jax.random.split(jax.random.key(seed), 9)
    part_splits = jax.random.split(jax.random.fold_in(streams_of[8], part), 9)
    innovations = gaussian(part_splits[0], (V, OBS), 1.0, 6.0, ((0, 2), (1, 8)), jnp.float32)
    obs_owner_keys = jax.random.split(jax.random.fold_in(part_splits[1], 1), OBS // OBS_DEV)
    obs_owner_turns = jax.random.permutation(jax.random.fold_in(part_splits[1], 3), OBS // OBS_DEV)
    obs_owner = jax.vmap(lambda own, number: deal_out(jax.random.fold_in(part_splits[1], 2), own, number, OBS_DEV, N_SUB, 1, CAP, 2))(obs_owner_keys, obs_owner_turns).reshape((OBS, 1))
    obs_local = with_ends(jax.random.randint(part_splits[2], (OBS,), 0, NX_DEV * NY), jax.random.fold_in(part_splits[2], 1), 0, (NX_DEV * NY) - 1).astype(jnp.int32)
    obs_level_keys = jax.random.split(jax.random.fold_in(part_splits[3], 1), OBS // OBS_DEV)
    obs_level_turns = jax.random.permutation(jax.random.fold_in(part_splits[3], 3), OBS // OBS_DEV)
    obs_level = jax.vmap(lambda own, number: deal_out(jax.random.fold_in(part_splits[3], 2), own, number, OBS_DEV, LEV, 1, LCAP, 1))(obs_level_keys, obs_level_turns).reshape((OBS, 1))
    band_width = with_ends(jax.random.randint(streams_of[4], (LEV,), 2, 4 * NX_DEV + 1), jax.random.fold_in(streams_of[4], 1), 2, 4 * NX_DEV).astype(jnp.int32)
    vert_scale = jnp.clip(jnp.exp(math.log(4.0) - 1.3862944 * jax.random.uniform(streams_of[5], (V, LEV), jnp.float32) ** block_levels(streams_of[5], (V, LEV), ((0, 2),), -0.2, 0.2)), 1.0, 4.0)
    sigma = jnp.clip(jnp.exp(math.log(2.0) - 1.3862944 * jax.random.uniform(streams_of[6], (V, LEV), jnp.float32) ** block_levels(streams_of[6], (V, LEV), ((0, 2),), -0.2, 0.2)), 0.5, 2.0)
    balance = draw_balance(jax.random.fold_in(streams_of[8], 71), part)
    return {"innovations": innovations, "obs_owner": obs_owner, "obs_local": obs_local, "obs_level": obs_level, "band_width": band_width, "vert_scale": vert_scale, "sigma": sigma, "balance": balance}


def filter_matrix(width, count):
    rate = width.astype(jnp.float32)[:, None, None]
    index = jnp.arange(count)
    dist = jnp.abs(index[:, None] - index[None, :]).astype(jnp.float32)
    far = (count - jnp.maximum(index[:, None], index[None, :])).astype(jnp.float32)
    return jnp.exp(-dist / rate) * (1.0 - jnp.exp(-2.0 * far / rate))


def vertical_matrix(scale):
    index = jnp.arange(LEV)
    dist = (index[:, None] - index[None, :]).astype(jnp.float32)
    corr = jnp.exp(-dist * dist / (2.0 * scale[:, :, None] * scale[:, None, :]))
    return jnp.where(jnp.abs(dist) <= VB, corr, jnp.float32(0.0))


def reference(innovations, obs_owner, obs_local, obs_level, band_width, vert_scale, sigma, balance):
    column_x = obs_owner[:, 0] * NX_DEV + obs_local // NY
    column_y = obs_local % NY
    flat = ((obs_level[:, 0] * NX + column_x) * NY + column_y).astype(jnp.int32)
    adjoint = jnp.zeros((V, LEV * NX * NY), jnp.float32).at[:, flat].add(innovations)
    adjoint = adjoint.reshape(V, LEV, NX, NY)
    across = filter_matrix(band_width, NX)
    along = filter_matrix(band_width, NY)
    high = lax.Precision.HIGHEST

    def per_level(packed):
        mat_x, mat_y, field = packed
        part = jnp.einsum("ij,vjy->viy", mat_x, field, precision=high)
        return jnp.einsum("vxj,yj->vxy", part, mat_y, precision=high)

    smoothed = lax.map(per_level, (across, along, jnp.transpose(adjoint, (1, 0, 2, 3))))
    smoothed = jnp.transpose(smoothed, (1, 0, 2, 3))
    corr = vertical_matrix(vert_scale)
    correlated = jnp.einsum("vlm,vmxy->vlxy", corr, smoothed, precision=high)
    mixed = jnp.einsum("vu,ulxy->vlxy", balance, correlated, precision=high)
    return mixed * sigma[:, :, None, None]
```

```python
import functools

import jax
import jax.numpy as jnp
from jax import lax
from jax.experimental import pallas as pl
from jax.experimental.pallas import tpu as pltpu
from jax.sharding import PartitionSpec as P

VB = 6
NX_DEV = 4
NY = 512
LCAP = 128
LANES = 128
BLOCKS = NY // LANES
TAPS = 2 * VB + 1
CHUNK = 8

NT = (((1,), (1,)), ((), ()))


def iota(shape, dim):
    return lax.broadcasted_iota(jnp.int32, shape, dim)


def split(x):
    high = x.astype(jnp.bfloat16)
    return high, (x - high.astype(jnp.float32)).astype(jnp.bfloat16)


def one_hot(count, value, width):
    number = iota((count, width), 0).astype(jnp.float32).astype(jnp.bfloat16)
    value = jnp.broadcast_to(value.astype(jnp.bfloat16), (count, width))
    return jnp.where(number == value, jnp.bfloat16(1), jnp.bfloat16(0))


def rank_own(levels, level_rows, spots, place):
    rows = level_rows.shape[0]
    lower = (iota((256, 256), 0) < iota((256, 256), 1)).astype(jnp.float32).astype(jnp.bfloat16)
    offset = jnp.zeros((levels, 1), jnp.float32)
    for at in range(0, rows, 2):
        level = jnp.concatenate([level_rows[at : at + 1, :], level_rows[at + 1 : at + 2, :]], axis=1)
        hits = (iota((levels, 256), 0) == level).astype(jnp.float32)
        before = jnp.dot(hits.astype(jnp.bfloat16), lower, preferred_element_type=jnp.float32)
        rank = jnp.sum(hits * (before + offset), axis=0, keepdims=True)
        offset = offset + jnp.sum(hits, axis=1, keepdims=True)
        slot = (level * LCAP + rank.astype(jnp.int32)) << 16
        place[at : at + 1, :] = slot[:, :LANES] + spots[at : at + 1, :]
        place[at + 1 : at + 2, :] = slot[:, LANES:] + spots[at + 1 : at + 2, :]


def bin_source(levels, table, bins, src, values, places, nvar):
    half = levels // 2
    rows = places.shape[1]
    per = 8
    for step in range(rows // per):
        lefts, rights = [], []
        for pair in range(per // 2):
            at = step * per + 2 * pair
            place = jnp.concatenate(
                [places[src, at : at + 1, :], places[src, at + 1 : at + 2, :]], axis=1
            )
            slot = place >> 16
            spot = place & 65535
            rights.append(
                one_hot(2 * LCAP, (slot & (2 * LCAP - 1)).astype(jnp.float32), 256)
            )
            pick = one_hot(half, (slot >> 8).astype(jnp.float32), 256)
            parts = []
            for v in range(nvar):
                parts += split(values[src, v : v + 1, at * LANES : (at + 2) * LANES])
            parts += [
                (spot >> 8).astype(jnp.float32).astype(jnp.bfloat16),
                (spot & 255).astype(jnp.float32).astype(jnp.bfloat16),
            ]
            lefts.append(jnp.concatenate([pick * part for part in parts], axis=0))
        left = jnp.concatenate(lefts, axis=1)
        right = jnp.concatenate(rights, axis=1)
        part = lax.dot_general(left, right, NT, preferred_element_type=jnp.float32)
        if step == 0:
            table[...] = part
        else:
            table[...] += part
    for parity in range(2):
        lanes = slice(parity * LCAP, (parity + 1) * LCAP)
        for v in range(nvar):
            at = 2 * v * half
            bins[src, parity, v] = (
                table[at : at + half, lanes] + table[at + half : at + 2 * half, lanes]
            )
        at = 2 * nvar * half
        spot = table[at : at + half, lanes] * 256.0 + table[at + half : at + 2 * half, lanes]
        spot = spot.astype(jnp.int32)
        bins[src, parity, nvar] = (spot >> 9).astype(jnp.float32)
        bins[src, parity, nvar + 1] = ((spot >> 7) & 3).astype(jnp.float32)
        bins[src, parity, nvar + 2] = (spot & 127).astype(jnp.float32)


def rate_of(band):
    return 1.0 / jnp.full((1, LANES), band.astype(jnp.float32), jnp.float32)


def add_level(groups, nvar, bins, pair, parity, rate, here):
    rows = nvar * NX_DEV
    wide = NX_DEV * groups
    near = (iota((8, LANES), 0) % NX_DEV + NX_DEV * here).astype(jnp.float32)
    which = iota((rows, LANES), 0) // NX_DEV
    total = None
    for first in range(0, groups, 8):
        lefts, rights = [], []
        for src in range(first, min(first + 8, groups)):
            def row(c):
                return bins[src, parity, c, pl.ds(pair, 1), :]

            x = row(nvar)
            gain = jnp.exp(-jnp.abs(near - x) * rate) * (
                1.0 - jnp.exp((-2.0 * rate) * (wide - jnp.maximum(near, x)))
            )
            gain = jnp.concatenate([gain] * (rows // 8), axis=0)
            value = row(nvar - 1)
            for v in range(nvar - 1):
                value = jnp.where(which == v, row(v), value)
            high, low = split(value * gain)
            block = jnp.broadcast_to(row(nvar + 1).astype(jnp.bfloat16), (rows, LANES))
            lefts.append(
                jnp.concatenate(
                    [
                        jnp.where(block == jnp.bfloat16(b), part, jnp.bfloat16(0))
                        for part in (high, low)
                        for b in range(BLOCKS)
                    ],
                    axis=0,
                )
            )
            rights.append(one_hot(LANES, row(nvar + 2), LANES))
        part = lax.dot_general(
            jnp.concatenate(lefts, axis=1),
            jnp.concatenate(rights, axis=1),
            NT,
            preferred_element_type=jnp.float32,
        )
        total = part if total is None else total + part
    size = BLOCKS * rows
    return total[:size] + total[size:]


def near_filter(rate):
    dist = jnp.abs(iota((LANES, LANES), 0) - iota((LANES, LANES), 1)).astype(jnp.float32)
    return jnp.concatenate(split(jnp.exp(-dist * rate)), axis=1)


def filter_level(nvar, total, near, rate, fields, level):
    rows = nvar * NX_DEV
    size = BLOCKS * rows
    quad = jnp.dot(
        jnp.concatenate(split(total), axis=0), near, preferred_element_type=jnp.float32
    )
    local = quad[:size, :LANES] + (quad[size:, :LANES] + quad[:size, LANES:])
    lane = iota((1, LANES), 1).astype(jnp.float32)
    to_end = jnp.exp((lane - (LANES - 1.0)) * rate)
    to_start = jnp.exp(-lane * rate)
    from_start = jnp.exp(-(lane + 1.0) * rate)
    from_end = jnp.exp((lane - float(LANES)) * rate)
    step = jnp.exp(-float(LANES) * rate)
    up = jnp.sum(total * to_end, axis=1, keepdims=True)
    down = jnp.sum(total * to_start, axis=1, keepdims=True)
    ups = [up[b * rows : (b + 1) * rows] for b in range(BLOCKS)]
    downs = [down[b * rows : (b + 1) * rows] for b in range(BLOCKS)]
    carry = [None] * BLOCKS
    for b in range(1, BLOCKS):
        carry[b] = ups[b - 1] if b == 1 else carry[b - 1] * step + ups[b - 1]
    edge = (carry[BLOCKS - 1] * step + ups[BLOCKS - 1]) * jnp.exp(-rate)
    back = [None] * BLOCKS
    back[BLOCKS - 1] = -edge
    for b in range(BLOCKS - 2, -1, -1):
        back[b] = back[b + 1] * step + downs[b + 1]
    for b in range(BLOCKS):
        out = local[b * rows : (b + 1) * rows] + back[b] * from_end
        if carry[b] is not None:
            out = out + carry[b] * from_start
        for v in range(nvar):
            fields[v, level + VB, b * NX_DEV : (b + 1) * NX_DEV, :] = out[
                v * NX_DEV : (v + 1) * NX_DEV
            ]


def kernel(
    groups, levels, nvar, value_ref, owner_ref, local_ref, level_ref, band_ref, scale_ref,
    sigma_ref, balance_ref, out_ref, values, places, place, table, bins, sums, filters, fields,
    mine, theirs, taps_vmem, taps, vsend, vrecv, psend, precv, swap_send, swap_recv, own_sem,
):
    here = lax.axis_index("sub")
    me = lax.axis_index("var")
    mesh_id = pl.DeviceIdType.MESH
    ranks = groups // 2
    line, side = here // 2, lax.rem(here, 2)
    twin = 2 * line + 1 - side
    barrier = pltpu.get_barrier_semaphore()
    friends = [2 * lax.rem(line + step, ranks) + side for step in range(1, ranks)]
    for peer in friends + [twin]:
        pl.semaphore_signal(barrier, inc=1, device_id={"sub": peer}, device_id_type=mesh_id)
    pl.semaphore_signal(barrier, inc=1, device_id={"var": 1 - me}, device_id_type=mesh_id)

    span = NX_DEV * NY
    rank_own(levels, level_ref, owner_ref[...] * span + local_ref[...], place)
    pl.semaphore_wait(barrier, ranks + 1)

    def send(slot, to, value_src, place_src):
        pair = []
        for source, target, out_sem, in_sem in (
            (value_src, values, vsend, vrecv), (place_src, places, psend, precv),
        ):
            copy = pltpu.make_async_remote_copy(
                src_ref=source, dst_ref=target.at[slot], send_sem=out_sem.at[slot],
                recv_sem=in_sem.at[slot], device_id={"sub": to}, device_id_type=mesh_id,
            )
            copy.start()
            pair.append(copy)
        return pair

    copies = {1: send(1, twin, value_ref, place)}
    for k, peer in enumerate(friends):
        copies[2 * k + 2] = send(2 * k + 2, peer, value_ref, place)
    own = [
        pltpu.make_async_copy(value_ref, values.at[0], own_sem.at[0]),
        pltpu.make_async_copy(place, places.at[0], own_sem.at[1]),
    ]
    for copy in own:
        copy.start()
    for copy in own:
        copy.wait()
    bin_source(levels, table, bins, 0, values, places, nvar)

    eye = iota((levels, levels), 0) == iota((levels, levels), 1)
    apart = (iota((levels, 2 * levels), 0) - iota((levels, 2 * levels), 1)).astype(jnp.float32)
    for v in range(nvar):
        across = scale_ref[v : v + 1, :]
        down = jnp.sum(jnp.where(eye, across, 0.0), axis=1, keepdims=True)
        across = jnp.concatenate([across, across], axis=1)
        taps_vmem[v * levels : (v + 1) * levels, :] = jnp.exp(
            -apart * apart / (2.0 * down * across)
        )
        fields[v, 0:VB] = jnp.zeros((VB,) + fields.shape[2:], jnp.float32)
        fields[v, VB + levels :] = jnp.zeros((VB,) + fields.shape[2:], jnp.float32)
    tap_copy = pltpu.make_async_copy(taps_vmem, taps, own_sem.at[2])
    tap_copy.start()

    def make_filter(quad, carry):
        for k in range(4):
            level = 4 * quad + k
            filters[level] = near_filter(rate_of(band_ref[level]))
        return carry

    lax.fori_loop(0, levels // 4, make_filter, 0)

    for k in range(1, ranks):
        for copy in copies[2 * k]:
            copy.wait_recv()
        copies[2 * k + 1] = send(2 * k + 1, twin, values.at[2 * k], places.at[2 * k])
        slot = 1 if k == 1 else 2 * k - 2
        if k == 1:
            for copy in copies[1]:
                copy.wait_recv()
        bin_source(levels, table, bins, slot, values, places, nvar)
    bin_source(levels, table, bins, 2 * ranks - 2, values, places, nvar)
    for k in range(1, ranks):
        for copy in copies[2 * k + 1]:
            copy.wait_recv()
        bin_source(levels, table, bins, 2 * k + 1, values, places, nvar)

    def add_pair(pair, carry):
        for parity in range(2):
            level = 2 * pair + parity
            rate = rate_of(band_ref[level])
            sums[level] = add_level(groups, nvar, bins, pair, parity, rate, here)
        return carry

    lax.fori_loop(0, levels // 2, add_pair, 0)

    def filter_four(quad, carry):
        for k in range(4):
            level = 4 * quad + k
            rate = rate_of(band_ref[level])
            filter_level(nvar, sums[level], filters[level], rate, fields, level)
        return carry

    lax.fori_loop(0, levels // 4, filter_four, 0)
    tap_copy.wait()

    swaps = []
    for chunk in range(levels // CHUNK):
        def correlate(k, carry, chunk=chunk):
            level = chunk * CHUNK + k
            for v in range(nvar):
                total = None
                for tap in range(TAPS):
                    other = jnp.clip(level + tap - VB, 0, levels - 1)
                    term = taps[v * levels + level, other] * fields[v, level + tap]
                    total = term if total is None else total + term
                mine[chunk, k, v] = total
            return carry

        lax.fori_loop(0, CHUNK, correlate, 0)
        swap = pltpu.make_async_remote_copy(
            src_ref=mine.at[chunk],
            dst_ref=theirs.at[chunk],
            send_sem=swap_send.at[chunk],
            recv_sem=swap_recv.at[chunk],
            device_id={"var": 1 - me},
            device_id_type=mesh_id,
        )
        swap.start()
        swaps.append(swap)
    for chunk in range(levels // CHUNK):
        swaps[chunk].wait_recv()

        def mix(k, carry, chunk=chunk):
            level = chunk * CHUNK + k
            first = [mine[chunk, k, u] for u in range(nvar)]
            second = [theirs[chunk, k, u] for u in range(nvar)]
            for v in range(nvar):
                total = None
                for u in range(nvar):
                    term = balance_ref[v, me * nvar + u] * first[u]
                    term = term + balance_ref[v, (1 - me) * nvar + u] * second[u]
                    total = term if total is None else total + term
                out_ref[v, level] = total * sigma_ref[v, level]
            return carry

        lax.fori_loop(0, CHUNK, mix, 0)
    for swap in swaps:
        swap.wait_send()
    for pair in copies.values():
        for copy in pair:
            copy.wait_send()


def on_device(innovations, obs_owner, obs_local, obs_level, band_width, vert_scale, sigma, balance):
    groups = lax.axis_size("sub")
    nvar, nobs = innovations.shape
    levels = band_width.shape[0]
    rows = BLOCKS * NX_DEV
    chunks = levels // CHUNK
    deep = nobs // LANES
    smem = pl.BlockSpec(memory_space=pltpu.SMEM)
    vmem = pl.BlockSpec(memory_space=pltpu.VMEM)
    out = pl.pallas_call(
        functools.partial(kernel, groups, levels, nvar),
        out_shape=jax.ShapeDtypeStruct((nvar, levels, rows, LANES), jnp.float32),
        in_specs=[vmem, vmem, vmem, vmem, smem, vmem, smem, smem],
        out_specs=vmem,
        scratch_shapes=[
            pltpu.VMEM((groups, nvar, nobs), jnp.float32),
            pltpu.VMEM((groups, deep, LANES), jnp.int32),
            pltpu.VMEM((deep, LANES), jnp.int32),
            pltpu.VMEM(((2 * nvar + 2) * levels // 2, 2 * LCAP), jnp.float32),
            pltpu.VMEM((groups, 2, nvar + 3, levels // 2, LCAP), jnp.float32),
            pltpu.VMEM((levels, nvar * rows, LANES), jnp.float32),
            pltpu.VMEM((levels, LANES, 2 * LANES), jnp.bfloat16),
            pltpu.VMEM((nvar, levels + 2 * VB, rows, LANES), jnp.float32),
            pltpu.VMEM((chunks, CHUNK, nvar, rows, LANES), jnp.float32),
            pltpu.VMEM((chunks, CHUNK, nvar, rows, LANES), jnp.float32),
            pltpu.VMEM((nvar * levels, 2 * levels), jnp.float32),
            pltpu.SMEM((nvar * levels, 2 * levels), jnp.float32),
            pltpu.SemaphoreType.DMA((groups,)),
            pltpu.SemaphoreType.DMA((groups,)),
            pltpu.SemaphoreType.DMA((groups,)),
            pltpu.SemaphoreType.DMA((groups,)),
            pltpu.SemaphoreType.DMA((chunks,)),
            pltpu.SemaphoreType.DMA((chunks,)),
            pltpu.SemaphoreType.DMA((3,)),
        ],
        compiler_params=pltpu.CompilerParams(
            collective_id=0, has_side_effects=True, vmem_limit_bytes=48 * 1024 * 1024
        ),
    )(
        innovations,
        obs_owner.reshape(deep, LANES),
        obs_local.reshape(deep, LANES),
        obs_level.reshape(deep, LANES),
        band_width,
        vert_scale,
        sigma,
        balance,
    )
    out = out.reshape(nvar, levels, BLOCKS, NX_DEV, LANES)
    return out.transpose(0, 1, 3, 2, 4).reshape(nvar, levels, NX_DEV, NY)


def solution(mesh):
    in_specs = (
        P("var", ("member", "sub")),
        P(("member", "sub"), None),
        P(("member", "sub")),
        P(("member", "sub"), None),
        P(),
        P("var", None),
        P("var", None),
        P("var", None),
    )
    out_specs = P("var", None, ("member", "sub"), None)
    return jax.shard_map(
        on_device, mesh=mesh, in_specs=in_specs, out_specs=out_specs, check_vma=False
    )
```

```python
import functools

import jax
import jax.numpy as jnp
from jax import lax
from jax.experimental import pallas as pl
from jax.experimental.pallas import tpu as pltpu
from jax.sharding import PartitionSpec as P

VB = 6
NX_DEV = 4
NY = 512
LCAP = 128
LANES = 128
BLOCKS = NY // LANES
TAPS = 2 * VB + 1
CHUNK = 8

NT = (((1,), (1,)), ((), ()))


def iota(shape, dim):
    return lax.broadcasted_iota(jnp.int32, shape, dim)


def split(x):
    high = x.astype(jnp.bfloat16)
    return high, (x - high.astype(jnp.float32)).astype(jnp.bfloat16)


def one_hot(count, value, width):
    number = iota((count, width), 0).astype(jnp.float32).astype(jnp.bfloat16)
    value = jnp.broadcast_to(value.astype(jnp.bfloat16), (count, width))
    return jnp.where(number == value, jnp.bfloat16(1), jnp.bfloat16(0))


def rank_own(levels, level_rows, spots, place):
    rows = level_rows.shape[0]
    lower = (iota((256, 256), 0) < iota((256, 256), 1)).astype(jnp.float32).astype(jnp.bfloat16)
    offset = jnp.zeros((levels, 1), jnp.float32)
    for at in range(0, rows, 2):
        level = jnp.concatenate([level_rows[at : at + 1, :], level_rows[at + 1 : at + 2, :]], axis=1)
        hits = (iota((levels, 256), 0) == level).astype(jnp.float32)
        before = jnp.dot(hits.astype(jnp.bfloat16), lower, preferred_element_type=jnp.float32)
        rank = jnp.sum(hits * (before + offset), axis=0, keepdims=True)
        offset = offset + jnp.sum(hits, axis=1, keepdims=True)
        slot = (level * LCAP + rank.astype(jnp.int32)) << 16
        place[at : at + 1, :] = slot[:, :LANES] + spots[at : at + 1, :]
        place[at + 1 : at + 2, :] = slot[:, LANES:] + spots[at + 1 : at + 2, :]


def bin_source(levels, table, bins, src, values, places, nvar):
    half = levels // 2
    rows = places.shape[1]
    per = 8
    for step in range(rows // per):
        lefts, rights = [], []
        for pair in range(per // 2):
            at = step * per + 2 * pair
            place = jnp.concatenate(
                [places[src, at : at + 1, :], places[src, at + 1 : at + 2, :]], axis=1
            )
            slot = place >> 16
            spot = place & 65535
            rights.append(
                one_hot(2 * LCAP, (slot & (2 * LCAP - 1)).astype(jnp.float32), 256)
            )
            pick = one_hot(half, (slot >> 8).astype(jnp.float32), 256)
            parts = []
            for v in range(nvar):
                parts += split(values[src, v : v + 1, at * LANES : (at + 2) * LANES])
            parts += [
                (spot >> 8).astype(jnp.float32).astype(jnp.bfloat16),
                (spot & 255).astype(jnp.float32).astype(jnp.bfloat16),
            ]
            lefts.append(jnp.concatenate([pick * part for part in parts], axis=0))
        left = jnp.concatenate(lefts, axis=1)
        right = jnp.concatenate(rights, axis=1)
        part = lax.dot_general(left, right, NT, preferred_element_type=jnp.float32)
        if step == 0:
            table[...] = part
        else:
            table[...] += part
    for parity in range(2):
        lanes = slice(parity * LCAP, (parity + 1) * LCAP)
        for v in range(nvar):
            at = 2 * v * half
            bins[src, parity, v] = (
                table[at : at + half, lanes] + table[at + half : at + 2 * half, lanes]
            )
        at = 2 * nvar * half
        spot = table[at : at + half, lanes] * 256.0 + table[at + half : at + 2 * half, lanes]
        spot = spot.astype(jnp.int32)
        bins[src, parity, nvar] = (spot >> 9).astype(jnp.float32)
        bins[src, parity, nvar + 1] = ((spot >> 7) & 3).astype(jnp.float32)
        bins[src, parity, nvar + 2] = (spot & 127).astype(jnp.float32)


def rate_of(band):
    return 1.0 / jnp.full((1, LANES), band.astype(jnp.float32), jnp.float32)


def add_level(groups, nvar, bins, pair, parity, rate, here):
    rows = nvar * NX_DEV
    wide = NX_DEV * groups
    near = (iota((8, LANES), 0) % NX_DEV + NX_DEV * here).astype(jnp.float32)
    which = iota((rows, LANES), 0) // NX_DEV
    total = None
    for first in range(0, groups, 8):
        lefts, rights = [], []
        for src in range(first, min(first + 8, groups)):
            def row(c):
                return bins[src, parity, c, pl.ds(pair, 1), :]

            x = row(nvar)
            gain = jnp.exp(-jnp.abs(near - x) * rate) * (
                1.0 - jnp.exp((-2.0 * rate) * (wide - jnp.maximum(near, x)))
            )
            gain = jnp.concatenate([gain] * (rows // 8), axis=0)
            value = row(nvar - 1)
            for v in range(nvar - 1):
                value = jnp.where(which == v, row(v), value)
            high, low = split(value * gain)
            block = jnp.broadcast_to(row(nvar + 1).astype(jnp.bfloat16), (rows, LANES))
            lefts.append(
                jnp.concatenate(
                    [
                        jnp.where(block == jnp.bfloat16(b), part, jnp.bfloat16(0))
                        for part in (high, low)
                        for b in range(BLOCKS)
                    ],
                    axis=0,
                )
            )
            rights.append(one_hot(LANES, row(nvar + 2), LANES))
        part = lax.dot_general(
            jnp.concatenate(lefts, axis=1),
            jnp.concatenate(rights, axis=1),
            NT,
            preferred_element_type=jnp.float32,
        )
        total = part if total is None else total + part
    size = BLOCKS * rows
    return total[:size] + total[size:]


def near_filter(rate):
    dist = jnp.abs(iota((LANES, LANES), 0) - iota((LANES, LANES), 1)).astype(jnp.float32)
    return jnp.concatenate(split(jnp.exp(-dist * rate)), axis=1)


def filter_level(nvar, total, near, rate, fields, level):
    rows = nvar * NX_DEV
    size = BLOCKS * rows
    quad = jnp.dot(
        jnp.concatenate(split(total), axis=0), near, preferred_element_type=jnp.float32
    )
    local = quad[:size, :LANES] + (quad[size:, :LANES] + quad[:size, LANES:])
    lane = iota((1, LANES), 1).astype(jnp.float32)
    to_end = jnp.exp((lane - (LANES - 1.0)) * rate)
    to_start = jnp.exp(-lane * rate)
    from_start = jnp.exp(-(lane + 1.0) * rate)
    from_end = jnp.exp((lane - float(LANES)) * rate)
    step = jnp.exp(-float(LANES) * rate)
    up = jnp.sum(total * to_end, axis=1, keepdims=True)
    down = jnp.sum(total * to_start, axis=1, keepdims=True)
    ups = [up[b * rows : (b + 1) * rows] for b in range(BLOCKS)]
    downs = [down[b * rows : (b + 1) * rows] for b in range(BLOCKS)]
    carry = [None] * BLOCKS
    for b in range(1, BLOCKS):
        carry[b] = ups[b - 1] if b == 1 else carry[b - 1] * step + ups[b - 1]
    edge = (carry[BLOCKS - 1] * step + ups[BLOCKS - 1]) * jnp.exp(-rate)
    back = [None] * BLOCKS
    back[BLOCKS - 1] = -edge
    for b in range(BLOCKS - 2, -1, -1):
        back[b] = back[b + 1] * step + downs[b + 1]
    for b in range(BLOCKS):
        out = local[b * rows : (b + 1) * rows] + back[b] * from_end
        if carry[b] is not None:
            out = out + carry[b] * from_start
        for v in range(nvar):
            fields[v, level + VB, b * NX_DEV : (b + 1) * NX_DEV, :] = out[
                v * NX_DEV : (v + 1) * NX_DEV
            ]


def kernel(
    groups, levels, nvar, value_hbm, owner_hbm, local_hbm, level_hbm, band_hbm, scale_hbm,
    sigma_hbm, balance_hbm, out_ref, value_ref, owner_ref, local_ref, level_ref, band_ref,
    scale_ref, sigma, balance, load_sem, values, places, place, table, bins, filters, fields,
    mine, theirs, taps_vmem, taps, vsend, vrecv, psend, precv, swap_send, swap_recv, own_sem,
):
    loads = [
        pltpu.make_async_copy(source, target, load_sem.at[k])
        for k, (source, target) in enumerate(
            [
                (owner_hbm, owner_ref), (local_hbm, local_ref), (level_hbm, level_ref),
                (value_hbm, value_ref), (band_hbm, band_ref), (scale_hbm, scale_ref),
                (sigma_hbm, sigma), (balance_hbm, balance),
            ]
        )
    ]
    for load in loads:
        load.start()
    here = lax.axis_index("sub")
    me = lax.axis_index("var")
    mesh_id = pl.DeviceIdType.MESH
    ranks = groups // 2
    rows = BLOCKS * NX_DEV
    line, side = here // 2, lax.rem(here, 2)
    twin = 2 * line + 1 - side
    barrier = pltpu.get_barrier_semaphore()
    friends = [2 * lax.rem(line + step, ranks) + side for step in range(1, ranks)]
    for peer in friends + [twin]:
        pl.semaphore_signal(barrier, inc=1, device_id={"sub": peer}, device_id_type=mesh_id)
    pl.semaphore_signal(barrier, inc=1, device_id={"var": 1 - me}, device_id_type=mesh_id)

    span = NX_DEV * NY
    for load in loads:
        load.wait()
    rank_own(levels, level_ref, owner_ref[...] * span + local_ref[...], place)
    pl.semaphore_wait(barrier, ranks + 1)

    def send(slot, to, value_src, place_src):
        pair = []
        for source, target, out_sem, in_sem in (
            (value_src, values, vsend, vrecv), (place_src, places, psend, precv),
        ):
            copy = pltpu.make_async_remote_copy(
                src_ref=source, dst_ref=target.at[slot], send_sem=out_sem.at[slot],
                recv_sem=in_sem.at[slot], device_id={"sub": to}, device_id_type=mesh_id,
            )
            copy.start()
            pair.append(copy)
        return pair

    copies = {1: send(1, twin, value_ref, place)}
    for k, peer in enumerate(friends):
        copies[2 * k + 2] = send(2 * k + 2, peer, value_ref, place)
    own = [
        pltpu.make_async_copy(value_ref, values.at[0], own_sem.at[0]),
        pltpu.make_async_copy(place, places.at[0], own_sem.at[1]),
    ]
    for copy in own:
        copy.start()
    for copy in own:
        copy.wait()
    bin_source(levels, table, bins, 0, values, places, nvar)

    eye = iota((levels, levels), 0) == iota((levels, levels), 1)
    apart = iota((levels, 2 * levels), 0) + VB - iota((levels, 2 * levels), 1)
    apart = apart.astype(jnp.float32)
    for v in range(nvar):
        across = scale_ref[v : v + 1, :]
        down = jnp.sum(jnp.where(eye, across, 0.0), axis=1, keepdims=True)
        across = jnp.concatenate([across[:, levels - VB :], across, across[:, : levels - VB]], axis=1)
        taps_vmem[v * levels : (v + 1) * levels, :] = jnp.exp(
            -apart * apart / (2.0 * down * across)
        )
        fields[v, 0:VB] = jnp.zeros((VB,) + fields.shape[2:], jnp.float32)
        fields[v, VB + levels :] = jnp.zeros((VB,) + fields.shape[2:], jnp.float32)
    tap_copy = pltpu.make_async_copy(taps_vmem, taps, own_sem.at[2])
    tap_copy.start()

    def make_filter(quad, carry):
        for k in range(4):
            level = 4 * quad + k
            filters[level] = near_filter(rate_of(band_ref[level]))
        return carry

    lax.fori_loop(0, levels // 4, make_filter, 0)

    for k in range(1, ranks):
        for copy in copies[2 * k]:
            copy.wait_recv()
        copies[2 * k + 1] = send(2 * k + 1, twin, values.at[2 * k], places.at[2 * k])
        slot = 1 if k == 1 else 2 * k - 2
        if k == 1:
            for copy in copies[1]:
                copy.wait_recv()
        bin_source(levels, table, bins, slot, values, places, nvar)
    bin_source(levels, table, bins, 2 * ranks - 2, values, places, nvar)
    for k in range(1, ranks):
        for copy in copies[2 * k + 1]:
            copy.wait_recv()
        bin_source(levels, table, bins, 2 * k + 1, values, places, nvar)

    def smooth_pair(pair, waiting):
        done = []
        for parity in range(2):
            level = 2 * pair - 2 + parity
            known = jnp.maximum(level, 0)
            filter_level(
                nvar, waiting[parity], filters[known], rate_of(band_ref[known]), fields, level
            )
            rate = rate_of(band_ref[2 * pair + parity])
            done.append(add_level(groups, nvar, bins, pair, parity, rate, here))
        return tuple(done)

    empty = jnp.zeros((nvar * rows, LANES), jnp.float32)
    last = lax.fori_loop(0, levels // 2, smooth_pair, (empty, empty))
    for parity in range(2):
        level = levels - 2 + parity
        filter_level(
            nvar, last[parity], filters[level], rate_of(band_ref[level]), fields, level
        )
    tap_copy.wait()

    swaps = []
    for chunk in range(levels // CHUNK):
        def correlate(quad, carry, chunk=chunk):
            for k in range(4):
                level = chunk * CHUNK + quad * 4 + k
                for v in range(nvar):
                    total = None
                    for tap in range(TAPS):
                        term = taps[v * levels + level, level + tap] * fields[v, level + tap]
                        total = term if total is None else total + term
                    mine[chunk, quad * 4 + k, v] = total
            return carry

        lax.fori_loop(0, CHUNK // 4, correlate, 0)
        swap = pltpu.make_async_remote_copy(
            src_ref=mine.at[chunk],
            dst_ref=theirs.at[chunk],
            send_sem=swap_send.at[chunk],
            recv_sem=swap_recv.at[chunk],
            device_id={"var": 1 - me},
            device_id_type=mesh_id,
        )
        swap.start()
        swaps.append(swap)
    for chunk in range(levels // CHUNK):
        swaps[chunk].wait_recv()

        def mix(quad, carry, chunk=chunk):
            for k in range(4):
                level = chunk * CHUNK + quad * 4 + k
                first = [mine[chunk, quad * 4 + k, u] for u in range(nvar)]
                second = [theirs[chunk, quad * 4 + k, u] for u in range(nvar)]
                for v in range(nvar):
                    total = None
                    for u in range(nvar):
                        term = balance[v, me * nvar + u] * first[u]
                        term = term + balance[v, (1 - me) * nvar + u] * second[u]
                        total = term if total is None else total + term
                    out_ref[v, level] = total * sigma[v, level]
            return carry

        lax.fori_loop(0, CHUNK // 4, mix, 0)
    for swap in swaps:
        swap.wait_send()
    for pair in copies.values():
        for copy in pair:
            copy.wait_send()


def on_device(innovations, obs_owner, obs_local, obs_level, band_width, vert_scale, sigma, balance):
    groups = lax.axis_size("sub")
    nvar, nobs = innovations.shape
    levels = band_width.shape[0]
    rows = BLOCKS * NX_DEV
    chunks = levels // CHUNK
    deep = nobs // LANES
    hbm = pl.BlockSpec(memory_space=pltpu.HBM)
    vmem = pl.BlockSpec(memory_space=pltpu.VMEM)
    out = pl.pallas_call(
        functools.partial(kernel, groups, levels, nvar),
        out_shape=jax.ShapeDtypeStruct((nvar, levels, rows, LANES), jnp.float32),
        in_specs=[hbm] * 8,
        out_specs=vmem,
        scratch_shapes=[
            pltpu.VMEM((nvar, nobs), jnp.float32),
            pltpu.VMEM((deep, LANES), jnp.int32),
            pltpu.VMEM((deep, LANES), jnp.int32),
            pltpu.VMEM((deep, LANES), jnp.int32),
            pltpu.SMEM((levels,), jnp.int32),
            pltpu.VMEM((nvar, levels), jnp.float32),
            pltpu.SMEM((nvar, levels), jnp.float32),
            pltpu.SMEM((nvar, 2 * nvar), jnp.float32),
            pltpu.SemaphoreType.DMA((8,)),
            pltpu.VMEM((groups, nvar, nobs), jnp.float32),
            pltpu.VMEM((groups, deep, LANES), jnp.int32),
            pltpu.VMEM((deep, LANES), jnp.int32),
            pltpu.VMEM(((2 * nvar + 2) * levels // 2, 2 * LCAP), jnp.float32),
            pltpu.VMEM((groups, 2, nvar + 3, levels // 2, LCAP), jnp.float32),
            pltpu.VMEM((levels, LANES, 2 * LANES), jnp.bfloat16),
            pltpu.VMEM((nvar, levels + 2 * VB, rows, LANES), jnp.float32),
            pltpu.VMEM((chunks, CHUNK, nvar, rows, LANES), jnp.float32),
            pltpu.VMEM((chunks, CHUNK, nvar, rows, LANES), jnp.float32),
            pltpu.VMEM((nvar * levels, 2 * levels), jnp.float32),
            pltpu.SMEM((nvar * levels, 2 * levels), jnp.float32),
            pltpu.SemaphoreType.DMA((groups,)),
            pltpu.SemaphoreType.DMA((groups,)),
            pltpu.SemaphoreType.DMA((groups,)),
            pltpu.SemaphoreType.DMA((groups,)),
            pltpu.SemaphoreType.DMA((chunks,)),
            pltpu.SemaphoreType.DMA((chunks,)),
            pltpu.SemaphoreType.DMA((3,)),
        ],
        compiler_params=pltpu.CompilerParams(
            collective_id=0, has_side_effects=True, vmem_limit_bytes=62 * 1024 * 1024
        ),
    )(
        innovations,
        obs_owner.reshape(deep, LANES),
        obs_local.reshape(deep, LANES),
        obs_level.reshape(deep, LANES),
        band_width,
        vert_scale,
        sigma,
        balance,
    )
    out = out.reshape(nvar, levels, BLOCKS, NX_DEV, LANES)
    return out.transpose(0, 1, 3, 2, 4).reshape(nvar, levels, NX_DEV, NY)


def solution(mesh):
    in_specs = (
        P("var", ("member", "sub")),
        P(("member", "sub"), None),
        P(("member", "sub")),
        P(("member", "sub"), None),
        P(),
        P("var", None),
        P("var", None),
        P("var", None),
    )
    out_specs = P("var", None, ("member", "sub"), None)
    return jax.shard_map(
        on_device, mesh=mesh, in_specs=in_specs, out_specs=out_specs, check_vma=False
    )
```
